32 devices in a mesh: frames: 4 (over y, core), blocks: 8 (over z, x).
Axes of the slice: x: 2, y: 2, z: 4, core: 2. Of those that a mesh axis runs over, the one named last changes fastest.
Arguments:
- traj: bfloat16 [4096, 8192], P('frames', 'blocks')
- span_offsets: int32 [4], replicated, may hold values from 0 to 256
- lag: int32 [1], replicated, may hold values from 1 to 256
- owner: int32 [36], replicated, may hold values from 0 to 7, as said below
Outputs:
- corr_inst: bfloat16 [40, 1024, 1024], P('blocks', 'frames')
- corr_lag: bfloat16 [40, 1024, 1024], P('blocks', 'frames')
The draws below stay inside these ranges and needn't reach their ends.
Inputs may be any that keep to these rules, and one draw needn't show every extreme that they name: At most 5 pairs share one owner, and some owner has exactly 5.
All inputs are finite; a program needn't handle non-finite values.
Results may differ from the reference program's by a relative error of at most 0.0059.
Values may be sent and summed in bfloat16 or wider, within the bound.
A program may use at most 192 MiB of HBM per device.

```python
import jax
import jax.numpy as jnp
import numpy as np
from jax import lax

NB = 8
BS = 1024
SPAN = 512
MAXLAG = 256
F = 8192
SEG = 1024
NPAIRS = 36
MAXOWN = 5
SLOTS = 40
N_FRAMES = 4
N_BLOCKS = 8


def smooth_sum(series):
    return series[:, 3:] + series[:, 2:-1] + series[:, 1:-2] + series[:, :-3]


def draw_traj(key, part):
    key = jax.random.fold_in(key, 11)
    keys = jax.random.split(key, 8)
    base = jax.random.uniform(keys[0], (F,), jnp.float32, -2.0, 2.0)
    scale = jnp.exp(jax.random.uniform(keys[1], (F,), jnp.float32, 0.0, 2.3))
    noise = jax.random.normal(keys[2], (N_FRAMES, SEG + 3, F), jnp.float32)
    latent = jax.random.normal(keys[3], (N_FRAMES, SEG + 3, 64), jnp.float32)
    shift = 0.8 * jax.random.normal(keys[4], (N_FRAMES, 1, F), jnp.float32)
    classes = jax.random.randint(keys[5], (F,), 0, 64)
    loading = jax.random.uniform(keys[6], (F,), jnp.float32, 0.5, 1.5)
    loading = loading * jnp.where(jax.random.randint(keys[7], (F,), 0, 2) == 0, -1.0, 1.0)
    noise = 0.5 * smooth_sum(noise)
    latent = 0.5 * smooth_sum(latent)
    amp = 0.4 + 1.6 * jnp.arange(SEG, dtype=jnp.float32) / SEG
    shared = jnp.take(latent, classes, axis=2) * amp[None, :, None]
    values = base + shift + scale * (noise + loading * shared)
    return values.reshape(N_FRAMES * SEG, F).astype(jnp.bfloat16)


def draw_owner(key, part):
    key = jax.random.fold_in(key, 23)
    first_key, second_key, third_key = jax.random.split(key, 3)
    total = N_BLOCKS * MAXOWN
    order_one = jax.random.permutation(first_key, total)
    position = jnp.argsort(order_one)
    chosen_dev = jax.random.randint(second_key, (), 0, N_BLOCKS)
    slot_ids = jnp.arange(total)
    score = position - total * (slot_ids // MAXOWN == chosen_dev).astype(jnp.int32)
    ordered = jnp.argsort(score, stable=True)
    picked = ordered[:NPAIRS] // MAXOWN
    shuffle = jax.random.permutation(third_key, NPAIRS)
    return picked[shuffle].astype(jnp.int32)


def place_ends(result, stream_key, least, top_value):
    longest = result.shape.index(max(result.shape))
    spots = []
    for shift in (0, 1):
        where = [jax.random.randint(jax.random.fold_in(stream_key, axis), (), 0, length) for axis, length in enumerate(result.shape)]
        where[longest] = (where[longest] + shift) % result.shape[longest]
        spots.append(tuple(where))
    return result.at[spots[0]].set(least).at[spots[1]].set(top_value)


def setup_inputs(seed: int = 0) -> dict:
    streams_of = jax.random.split(jax.random.key(seed), 5)
    return {
        "traj": draw_traj(jax.random.fold_in(streams_of[4], 71), 0),
        "span_offsets": place_ends(jax.random.randint(streams_of[1], (N_FRAMES,), 0, SPAN - MAXLAG + 1), jax.random.fold_in(streams_of[1], 1), 0, SPAN - MAXLAG).astype(jnp.int32),
        "lag": jax.random.randint(streams_of[2], (1,), 1, MAXLAG + 1).astype(jnp.int32),
        "owner": draw_owner(jax.random.fold_in(streams_of[4], 71), 0),
    }


eps = 1e-06

def reference(traj, span_offsets, lag, owner):
    segments = traj.reshape(N_FRAMES, SEG, F)

    def pick(segment, offset):
        start = offset.astype(jnp.int32)
        first = lax.dynamic_slice_in_dim(segment, start, SPAN, 0)
        later = lax.dynamic_slice_in_dim(segment, (start + lag[0]).astype(jnp.int32), SPAN, 0)
        return (first, later)
    first, later = jax.vmap(pick)(segments, span_offsets)
    first = first.astype(jnp.float32).reshape(N_FRAMES * SPAN, F)
    later = later.astype(jnp.float32).reshape(N_FRAMES * SPAN, F)
    count = N_FRAMES * SPAN
    cent0 = (first - lax.optimization_barrier(jnp.sum(first, 0)) / count).astype(jnp.bfloat16)
    cent1 = (later - lax.optimization_barrier(jnp.sum(later, 0)) / count).astype(jnp.bfloat16)
    squares = lax.optimization_barrier(jnp.sum(jnp.square(cent0.astype(jnp.float32)), 0))
    inv = 1.0 / jnp.sqrt(squares + eps)
    s00 = jnp.dot(cent0.T, cent0, preferred_element_type=jnp.float32)
    s01 = jnp.dot(cent0.T, cent1, preferred_element_type=jnp.float32)
    k00 = s00 * inv[:, None] * inv[None, :]
    k01 = 0.5 * (s01 + s01.T) * inv[:, None] * inv[None, :]
    rows_np, cols_np = np.triu_indices(NB)
    block00 = k00.reshape(NB, BS, NB, BS)[rows_np, :, cols_np, :]
    block01 = k01.reshape(NB, BS, NB, BS)[rows_np, :, cols_np, :]
    same_owner = (owner[:, None] == owner[None, :]).astype(jnp.int32)
    before = jnp.asarray(np.tril(np.ones((NPAIRS, NPAIRS), np.int32), -1))
    rank = lax.optimization_barrier(jnp.sum(same_owner * before, 1)).astype(jnp.int32)
    slot = (owner * MAXOWN + rank).astype(jnp.int32)
    corr_inst = jnp.zeros((SLOTS, BS, BS), jnp.float32).at[slot].set(block00)
    corr_lag = jnp.zeros((SLOTS, BS, BS), jnp.float32).at[slot].set(block01)
    return (corr_inst.astype(jnp.bfloat16), corr_lag.astype(jnp.bfloat16))
```

```python
import functools

import jax
import jax.numpy as jnp
import numpy as np
from jax import lax
from jax.experimental import pallas as pl
from jax.experimental.pallas import tpu as pltpu
from jax.sharding import PartitionSpec as P

BS = 1024
SPAN = 512
MAXLAG = 256
WINDOW = SPAN + MAXLAG
ZX_PIECES = ((0, 320), (320, 320))
XZ_PIECE = (640, 128)
eps = 1e-06
MESH = pl.DeviceIdType.MESH


def remote(src, dst, send_sem, recv_sem, device_id):
    return pltpu.make_async_remote_copy(
        src_ref=src,
        dst_ref=dst,
        send_sem=send_sem,
        recv_sem=recv_sem,
        device_id=device_id,
        device_id_type=MESH,
    )


def gather_kernel(
    nz, lag_ref, raw_ref, gat_ref, stats_ref,
    sums, squares, send_sem, recv_sem, own_sem,
    sum_send, sum_recv, sq_send, sq_recv, st_send, st_recv,
):
    nf = lax.axis_size("frames")
    nb = 2 * nz
    group = lax.axis_index("frames")
    me = lax.axis_index("blocks")
    z, x = me // 2, me % 2
    across = z * 2 + 1 - x
    width = raw_ref.shape[1]

    barrier = pltpu.get_barrier_semaphore()
    for d in range(1, nb):
        pl.semaphore_signal(
            barrier, inc=1, device_id={"blocks": (me + d) % nb}, device_id_type=MESH
        )
    for d in range(1, nf):
        pl.semaphore_signal(
            barrier, inc=1, device_id={"frames": (group + d) % nf}, device_id_type=MESH
        )
    pl.semaphore_wait(barrier, nb + nf - 2)

    pending = []
    pieces = ZX_PIECES + (XZ_PIECE,)

    def send(cond, block, k, way, target):
        start, size = pieces[k]
        rows = pl.ds(start, size)

        def copy(src):
            return remote(
                src,
                gat_ref.at[block, rows],
                send_sem.at[way, block, k],
                recv_sem.at[block, k],
                {"blocks": target},
            )

        mine = block is me
        src = raw_ref.at[rows] if mine else gat_ref.at[block, rows]

        def go():
            copy(src).start()

        def end():
            copy(src).wait_send()

        if cond is None:
            go()
        else:
            pl.when(cond)(go)
        pending.append((cond, end))

    def arrived(block, k):
        start, size = pieces[k]
        here = gat_ref.at[block, pl.ds(start, size)]
        pltpu.make_async_copy(here, here, recv_sem.at[block, k]).wait()

    up, down = me + 2, me - 2
    send(None, me, 2, 2, across)
    for k in range(len(pieces)):
        send(z < nz - 1, me, k, 0, up)
        send(z > 0, me, k, 1, down)
        if k < 2:
            send(None, me, k, 2, across)
    own = pltpu.make_async_copy(raw_ref, gat_ref.at[me], own_sem)
    own.start()

    lag = lag_ref[0]
    chunk = 64
    zero = jnp.zeros((1, width), jnp.float32)

    def add(i, carry):
        total0, total1 = carry
        start = pl.multiple_of(i * chunk, chunk)
        values = raw_ref[pl.ds(start, chunk), :].astype(jnp.float32)
        row = start + lax.broadcasted_iota(jnp.int32, (chunk, width), 0)
        in0 = row < SPAN
        in1 = (row >= lag) & (row < lag + SPAN)
        total0 += jnp.sum(jnp.where(in0, values, 0.0), 0, keepdims=True)
        total1 += jnp.sum(jnp.where(in1, values, 0.0), 0, keepdims=True)
        return total0, total1

    total0, total1 = lax.fori_loop(0, WINDOW // chunk, add, (zero, zero))
    sums[group] = jnp.concatenate([total0, total1, jnp.zeros((6, width), jnp.float32)], 0)

    def spread(buf, ssem, rsem):
        copies = []
        for d in range(1, nf):
            other = (group + d) % nf
            copy = remote(
                buf.at[group], buf.at[group], ssem.at[d], rsem.at[d], {"frames": other}
            )
            copy.start()
            copies.append(copy)
        return copies

    sum_copies = spread(sums, sum_send, sum_recv)

    arrived(across, 2)
    send(z < nz - 1, across, 2, 0, up)
    send(z > 0, across, 2, 1, down)

    def forward(dist):
        for k in range(2):
            for side in (-1, 1):
                zb = z + side * dist
                have = (zb >= 0) if side < 0 else (zb < nz)
                block = zb * 2 + x
                on = have & ((z < nz - 1) if side < 0 else (z > 0))
                pl.when(have)(functools.partial(arrived, block, k))
                send(on, block, k, 0 if side < 0 else 1, up if side < 0 else down)
                send(have, block, k, 2, across)
        for side in (-1, 1):
            zb = z + side * dist
            have = (zb >= 0) if side < 0 else (zb < nz)
            on = have & ((z < nz - 1) if side < 0 else (z > 0))
            for block in (zb * 2 + x, zb * 2 + 1 - x):
                pl.when(have)(functools.partial(arrived, block, 2))
                send(on, block, 2, 0 if side < 0 else 1, up if side < 0 else down)

    forward(1)
    for copy in sum_copies:
        copy.wait()
    means = sums[0]
    for i in range(1, nf):
        means = means + sums[i]
    means = means / (nf * SPAN)
    mean0 = means[0:1]

    def add_squares(i, total):
        start = pl.multiple_of(i * chunk, chunk)
        values = raw_ref[pl.ds(start, chunk), :].astype(jnp.float32)
        cent = (values - mean0).astype(jnp.bfloat16).astype(jnp.float32)
        return total + jnp.sum(cent * cent, 0, keepdims=True)

    total = lax.fori_loop(0, SPAN // chunk, add_squares, zero)
    squares[group] = jnp.broadcast_to(total, (8, width))
    sq_copies = spread(squares, sq_send, sq_recv)
    forward(2)
    for copy in sq_copies:
        copy.wait()
    total = squares[0]
    for i in range(1, nf):
        total = total + squares[i]
    row = lax.broadcasted_iota(jnp.int32, (8, width), 0)
    stats_ref[me] = jnp.where(row < 2, means, total)
    st_copies = []
    for d in range(1, nb):
        copy = remote(
            stats_ref.at[me], stats_ref.at[me], st_send.at[d], st_recv.at[d],
            {"blocks": (me + d) % nb},
        )
        copy.start()
        st_copies.append(copy)
    for dist in range(3, nz):
        forward(dist)
    for k in range(2):
        arrived(across, k)
    for dist in range(1, nz):
        for side in (-1, 1):
            zb = z + side * dist
            have = (zb >= 0) if side < 0 else (zb < nz)
            for k in range(2):
                pl.when(have)(functools.partial(arrived, zb * 2 + 1 - x, k))
    for cond, end in pending:
        if cond is None:
            end()
        else:
            pl.when(cond)(end)
    for copy in st_copies:
        copy.wait()
    own.wait()


def gather_windows(raw, lag):
    nf = lax.axis_size("frames")
    nb = lax.axis_size("blocks")
    width = raw.shape[1]
    dma = pltpu.SemaphoreType.DMA
    return pl.pallas_call(
        functools.partial(gather_kernel, nb // 2),
        out_shape=(
            jax.ShapeDtypeStruct((nb, WINDOW, width), jnp.bfloat16),
            jax.ShapeDtypeStruct((nb, 8, width), jnp.float32),
        ),
        in_specs=[
            pl.BlockSpec(memory_space=pltpu.SMEM),
            pl.BlockSpec(memory_space=pltpu.VMEM),
        ],
        out_specs=(
            pl.BlockSpec(memory_space=pl.ANY),
            pl.BlockSpec(memory_space=pltpu.VMEM),
        ),
        scratch_shapes=[
            pltpu.VMEM((nf, 8, width), jnp.float32),
            pltpu.VMEM((nf, 8, width), jnp.float32),
            dma((3, nb, 3)),
            dma((nb, 3)),
            dma,
            dma((nf,)),
            dma((nf,)),
            dma((nf,)),
            dma((nf,)),
            dma((nb,)),
            dma((nb,)),
        ],
        compiler_params=pltpu.CompilerParams(
            collective_id=0, has_side_effects=True, vmem_limit_bytes=32 * 2**20
        ),
        name="gather_windows",
    )(lag, raw)


def products_kernel(
    maxown, table_ref, full0_ref, full1_ref, out_ref,
    core_send, core_recv, held, y_send, y_recv,
    cs_sem, cr_sem, ys_sem, yr_sem,
):
    group = lax.axis_index("frames")
    y, core = group // 2, group % 2
    mate = y * 2 + 1 - core
    far = (1 - y) * 2 + core
    quarter = BS // 4
    barrier = pltpu.get_barrier_semaphore()
    for other in (mate, far):
        pl.semaphore_signal(barrier, inc=1, device_id={"frames": other}, device_id_type=MESH)
    pl.semaphore_wait(barrier, 2)
    contract = (((0,), (0,)), ((), ()))

    def dot(a, b):
        return lax.dot_general(a, b, contract, preferred_element_type=jnp.float32)

    def core_copy(t, part):
        return remote(
            core_send.at[t % 4, part], core_recv.at[t, part],
            cs_sem.at[t % 4, part], cr_sem.at[t, part], {"frames": mate},
        )

    def y_copy(t):
        return remote(
            y_send.at[t % 4], y_recv.at[t], ys_sem.at[t % 4], yr_sem.at[t], {"frames": far}
        )

    def multiply(s):
        i = table_ref[0, s]
        j = table_ref[1, s]

        def part(row_quarter, store):
            cols = pl.ds(pl.multiple_of(row_quarter * quarter, quarter), quarter)
            left0 = full0_ref[i, :, cols]
            left1 = full1_ref[i, :, cols]
            store(0, dot(left0, full0_ref[j]))
            store(1, dot(left0, full1_ref[j]) + dot(left1, full0_ref[j]))

        for p, row_quarter in enumerate(((1 - y) * 2 + 1 - core, y * 2 + 1 - core)):
            def to_mate(o, value, p=p):
                t = s * 2 + o

                @pl.when(s >= 2)
                def _():
                    core_copy(t, p).wait_send()

                core_send[t % 4, p] = value.astype(jnp.bfloat16)
                core_copy(t, p).start()

            part(row_quarter, to_mate)

        def keep_far(o, value):
            held[(s % 2) * 2 + o] = value

        def keep_mine(o, value):
            out_ref[s * 2 + o] = value

        part((1 - y) * 2 + core, keep_far)
        part(y * 2 + core, keep_mine)

    def pass_on(s):
        for o in range(2):
            t = s * 2 + o
            core_copy(t, 0).wait_recv()
            core_copy(t, 1).wait_recv()

            @pl.when(s >= 2)
            def _():
                y_copy(t).wait_send()

            y_send[t % 4] = (
                held[(s % 2) * 2 + o] + core_recv[t, 0].astype(jnp.float32)
            ).astype(jnp.bfloat16)
            y_copy(t).start()
            out_ref[t] += core_recv[t, 1].astype(jnp.float32)

    def step(s, carry):
        pl.when(s < maxown)(lambda: multiply(s))
        pl.when(s >= 1)(lambda: pass_on(s - 1))
        return carry

    lax.fori_loop(0, maxown + 1, step, 0)

    def finish(t, carry):
        y_copy(t).wait_recv()
        out_ref[t] += y_recv[t].astype(jnp.float32)
        return carry

    lax.fori_loop(0, 2 * maxown, finish, 0)
    for t in range(max(0, 2 * maxown - 4), 2 * maxown):
        y_copy(t).wait_send()
        core_copy(t, 0).wait_send()
        core_copy(t, 1).wait_send()


def owned_products(table, full0, full1, maxown):
    quarter = BS // 4
    n = 2 * maxown
    dma = pltpu.SemaphoreType.DMA
    vmem = pl.BlockSpec(memory_space=pltpu.VMEM)
    return pl.pallas_call(
        functools.partial(products_kernel, maxown),
        out_shape=jax.ShapeDtypeStruct((n, quarter, BS), jnp.float32),
        in_specs=[pl.BlockSpec(memory_space=pltpu.SMEM), vmem, vmem],
        out_specs=vmem,
        scratch_shapes=[
            pltpu.VMEM((4, 2, quarter, BS), jnp.bfloat16),
            pltpu.VMEM((n, 2, quarter, BS), jnp.bfloat16),
            pltpu.VMEM((4, quarter, BS), jnp.float32),
            pltpu.VMEM((4, quarter, BS), jnp.bfloat16),
            pltpu.VMEM((n, quarter, BS), jnp.bfloat16),
            dma((4, 2)),
            dma((n, 2)),
            dma((4,)),
            dma((n,)),
        ],
        compiler_params=pltpu.CompilerParams(
            collective_id=1, has_side_effects=True, vmem_limit_bytes=60 * 2**20
        ),
        name="owned_products",
    )(table, full0, full1)


def gather_plain(raw, lag):
    nframes = lax.axis_size("frames")
    count = nframes * SPAN
    first = raw[:SPAN].astype(jnp.float32)
    later = lax.dynamic_slice_in_dim(raw, lag, SPAN, 0).astype(jnp.float32)
    means = lax.psum(jnp.stack([jnp.sum(first, 0), jnp.sum(later, 0)]), "frames") / count
    cent0 = (first - means[0]).astype(jnp.bfloat16)
    own = lax.psum(jnp.sum(jnp.square(cent0.astype(jnp.float32)), 0), "frames")
    stats = jnp.concatenate([means, own[None]], 0)
    return lax.all_gather(raw, "blocks", axis=0), lax.all_gather(stats, "blocks", axis=0)


def shards(traj, span_offsets, lag, owner):
    nframes = lax.axis_size("frames")
    nblocks = lax.axis_size("blocks")
    group = lax.axis_index("frames")
    device = lax.axis_index("blocks")
    width = traj.shape[1] * nblocks
    nfeat = width // BS
    quarter = BS // nframes
    offset = jnp.sum(jnp.where(jnp.arange(nframes) == group, span_offsets, 0))
    raw = lax.dynamic_slice_in_dim(traj, offset, WINDOW, 0)
    if nblocks == 8 and nframes == 4:
        gathered, stats = gather_windows(raw, lag)
    else:
        gathered, stats = gather_plain(raw, lag[0])
        split = (nfeat, nblocks // nfeat)
        gathered = gathered.reshape(split + gathered.shape[1:])
        gathered = jnp.swapaxes(gathered, 1, 2).reshape(nfeat, WINDOW, BS)
        stats = stats.reshape(split + stats.shape[1:])
        stats = jnp.swapaxes(stats, 1, 2).reshape(nfeat, stats.shape[2], BS)
    full0 = (gathered[:, :SPAN].astype(jnp.float32) - stats[:, 0:1]).astype(jnp.bfloat16)
    full1 = lax.dynamic_slice_in_dim(gathered, lag[0], SPAN, 1).astype(jnp.float32)
    full1 = (full1 - stats[:, 1:2]).astype(jnp.bfloat16)
    inv = 1.0 / jnp.sqrt(stats[:, 2] + eps)

    rows_np, cols_np = np.triu_indices(nfeat)
    npairs = rows_np.shape[0]
    maxown = (npairs + nblocks - 1) // nblocks
    before = jnp.asarray(np.tril(np.ones((npairs, npairs), np.int32), -1))
    mine = owner == device
    rank = jnp.sum(before * mine.astype(jnp.int32)[None, :], 1)
    selected = mine[None, :] & (rank[None, :] == jnp.arange(maxown)[:, None])
    present = jnp.any(selected, 1)
    row_block = jnp.sum(jnp.where(selected, jnp.asarray(rows_np.astype(np.int32)), 0), 1)
    col_block = jnp.sum(jnp.where(selected, jnp.asarray(cols_np.astype(np.int32)), 0), 1)
    table = jnp.stack([row_block, col_block]).astype(jnp.int32)

    total = owned_products(table, full0, full1, maxown)
    total = total.reshape(maxown, 2, quarter, BS)
    mine_inv = lax.dynamic_slice_in_dim(inv, group * quarter, quarter, 1)
    row_inv = jnp.where(present[:, None], jnp.take(mine_inv, row_block, axis=0), 0.0)
    col_inv = jnp.take(inv, col_block, axis=0)
    corr_inst = total[:, 0] * row_inv[:, :, None] * col_inv[:, None, :]
    corr_lag = 0.5 * total[:, 1] * row_inv[:, :, None] * col_inv[:, None, :]
    return (corr_inst.astype(jnp.bfloat16), corr_lag.astype(jnp.bfloat16))


def solution(mesh):
    in_specs = (P("frames", "blocks"), P(), P(), P())
    out_specs = (P("blocks", "frames", None), P("blocks", "frames", None))
    return jax.shard_map(shards, mesh=mesh, in_specs=in_specs, out_specs=out_specs, check_vma=False)
```

```python
import functools

import jax
import jax.numpy as jnp
import numpy as np
from jax import lax
from jax.experimental import pallas as pl
from jax.experimental.pallas import tpu as pltpu
from jax.sharding import PartitionSpec as P

BS = 1024
SPAN = 512
MAXLAG = 256
WINDOW = SPAN + MAXLAG
CHUNKS = 2
ZX_PIECES = ((0, 320), (320, 320))
XZ_PIECE = (640, 128)
eps = 1e-06
MESH = pl.DeviceIdType.MESH


def remote(src, dst, send_sem, recv_sem, device_id):
    return pltpu.make_async_remote_copy(
        src_ref=src,
        dst_ref=dst,
        send_sem=send_sem,
        recv_sem=recv_sem,
        device_id=device_id,
        device_id_type=MESH,
    )


def shells():
    tiles = []
    for p in range(CHUNKS):
        tiles += [(p, c) for c in range(p + 1)] + [(r, p) for r in range(p)]
    return tiles


def fused_kernel(
    nz, maxown, lag_ref, table_ref, raw_ref, out_ref, stats_ref,
    sums, squares, shift, left, right, prod,
    core_send, core_recv, held, y_send, y_recv,
    send_sem, recv_sem, own_sem,
    sum_send, sum_recv, sq_send, sq_recv, st_send, st_recv,
    cs_sem, cr_sem, ys_sem, yr_sem, *gat,
):
    nf = lax.axis_size("frames")
    nb = 2 * nz
    group = lax.axis_index("frames")
    me = lax.axis_index("blocks")
    z, x = me // 2, me % 2
    y, core = group // 2, group % 2
    mate = y * 2 + 1 - core
    far = (1 - y) * 2 + core
    across = z * 2 + 1 - x
    chunk_width = raw_ref.shape[2]
    rows = chunk_width // 4

    barrier = pltpu.get_barrier_semaphore()
    for d in range(1, nb):
        pl.semaphore_signal(
            barrier, inc=1, device_id={"blocks": (me + d) % nb}, device_id_type=MESH
        )
    for d in range(1, nf):
        pl.semaphore_signal(
            barrier, inc=1, device_id={"frames": (group + d) % nf}, device_id_type=MESH
        )
    pl.semaphore_wait(barrier, nb + nf - 2)

    pending = []
    last = len(ZX_PIECES)
    pieces = ZX_PIECES + (XZ_PIECE,)

    def send(cond, h, block, k, way, target):
        start, size = pieces[k]
        span = pl.ds(start, size)
        src = raw_ref.at[h, span] if block is me else gat[h].at[block, span]

        def copy():
            return remote(
                src,
                gat[h].at[block, span],
                send_sem.at[way, block, h, k],
                recv_sem.at[block, h, k],
                {"blocks": target},
            )

        def go():
            copy().start()

        def end():
            copy().wait_send()

        if cond is None:
            go()
        else:
            pl.when(cond)(go)
        pending.append((cond, end))

    def arrived(h, block, k):
        start, size = pieces[k]
        here = gat[h].at[block, pl.ds(start, size)]
        pltpu.make_async_copy(here, here, recv_sem.at[block, h, k]).wait()

    up, down = me + 2, me - 2
    is_up, is_down = z < nz - 1, z > 0

    def start_own(h):
        send(None, h, me, last, 2, across)
        for k in range(last + 1):
            send(is_up, h, me, k, 0, up)
            send(is_down, h, me, k, 1, down)
            if k < last:
                send(None, h, me, k, 2, across)

    def pass_across(h):
        arrived(h, across, last)
        send(is_up, h, across, last, 0, up)
        send(is_down, h, across, last, 1, down)

    def forward(h, dist):
        for k in range(last):
            for side in (-1, 1):
                zb = z + side * dist
                have = (zb >= 0) if side < 0 else (zb < nz)
                block = zb * 2 + x
                on = have & (is_up if side < 0 else is_down)
                pl.when(have)(functools.partial(arrived, h, block, k))
                send(on, h, block, k, 0 if side < 0 else 1, up if side < 0 else down)
                send(have, h, block, k, 2, across)
        for side in (-1, 1):
            zb = z + side * dist
            have = (zb >= 0) if side < 0 else (zb < nz)
            on = have & (is_up if side < 0 else is_down)
            for block in (zb * 2 + x, zb * 2 + 1 - x):
                pl.when(have)(functools.partial(arrived, h, block, last))
                send(on, h, block, last, 0 if side < 0 else 1, up if side < 0 else down)

    def rest(h):
        for k in range(last):
            arrived(h, across, k)
        for dist in range(1, nz):
            for side in (-1, 1):
                zb = z + side * dist
                have = (zb >= 0) if side < 0 else (zb < nz)
                for k in range(last):
                    pl.when(have)(functools.partial(arrived, h, zb * 2 + 1 - x, k))

    def core_copy(p, t, part):
        n = 2 * p + 1
        return remote(
            core_send.at[t % 4, part, pl.ds(0, n)],
            core_recv.at[t, part, pl.ds(p * p, n)],
            cs_sem.at[t % 4, part], cr_sem.at[p, t, part], {"frames": mate},
        )

    def y_copy(p, t):
        n = 2 * p + 1
        return remote(
            y_send.at[t, pl.ds(0, n)], y_recv.at[t, pl.ds(p * p, n)],
            ys_sem.at[t], yr_sem.at[p, t], {"frames": far},
        )

    tiles = shells()
    contract = (((0,), (0,)), ((), ()))

    def dot(a, b):
        return lax.dot_general(a, b, contract, preferred_element_type=jnp.float32)

    def center(block, h, target, first, second):
        base = gat[h][block, pl.ds(0, SPAN)].astype(jnp.float32)
        target[h, pl.ds(first, SPAN)] = (base - stats_ref[block, h, 0:1]).astype(jnp.bfloat16)
        later = jnp.dot(shift[...], gat[h][block], preferred_element_type=jnp.float32)
        target[h, pl.ds(second, SPAN)] = (later - stats_ref[block, h, 1:2]).astype(jnp.bfloat16)

    def multiply(p, s):
        i = table_ref[0, s]
        j = table_ref[1, s]
        for h in range(p + 1):
            center(i, h, left, 0, SPAN)
            center(j, h, right, SPAN, 0)

        @pl.when(s >= 2)
        def _():
            for o in range(2):
                for part in range(2):
                    core_copy(p, s * 2 + o, part).wait_send()

        for o in range(2):
            t = s * 2 + o
            for n in range(2 * p + 1):
                r, c = tiles[p * p + n]
                if o == 0:
                    prod[...] = dot(left[r, 0:SPAN], right[c, SPAN : 2 * SPAN])
                else:
                    prod[...] = dot(left[r], right[c])

                def quarter(q):
                    return prod[pl.ds(pl.multiple_of(q * rows, rows), rows)]

                core_send[t % 4, 0, n] = quarter((1 - y) * 2 + 1 - core).astype(jnp.bfloat16)
                core_send[t % 4, 1, n] = quarter(y * 2 + 1 - core).astype(jnp.bfloat16)
                held[t % 4, n] = quarter((1 - y) * 2 + core)
                out_ref[t, p * p + n] = quarter(y * 2 + core)
            core_copy(p, t, 0).start()
            core_copy(p, t, 1).start()

    def pass_on(p, s):
        span = pl.ds(p * p, 2 * p + 1)
        for o in range(2):
            t = s * 2 + o
            core_copy(p, t, 0).wait_recv()
            core_copy(p, t, 1).wait_recv()
            y_send[t, pl.ds(0, 2 * p + 1)] = (
                held[t % 4, pl.ds(0, 2 * p + 1)] + core_recv[t, 0, span].astype(jnp.float32)
            ).astype(jnp.bfloat16)
            y_copy(p, t).start()
            out_ref[t, span] += core_recv[t, 1, span].astype(jnp.float32)

    def compute(p, low, high):
        def step(s, carry):
            pl.when(s < maxown)(lambda: multiply(p, s))
            pl.when(s >= 1)(lambda: pass_on(p, s - 1))
            return carry

        lax.fori_loop(low, high, step, 0)

    def drain(p):
        for t in range(max(0, 2 * maxown - 4), 2 * maxown):
            core_copy(p, t, 0).wait_send()
            core_copy(p, t, 1).wait_send()
        for t in range(2 * maxown):
            y_copy(p, t).wait_send()

    start_own(0)
    own = [
        pltpu.make_async_copy(raw_ref.at[h], gat[h].at[me], own_sem.at[h]) for h in range(CHUNKS)
    ]
    for copy in own:
        copy.start()
    lag = lag_ref[0]
    step_rows = 64
    shape = (step_rows, chunk_width)
    zero = jnp.zeros((1, chunk_width), jnp.float32)
    for h in range(CHUNKS):

        def add(i, carry, h=h):
            total0, total1 = carry
            start = pl.multiple_of(i * step_rows, step_rows)
            values = raw_ref[h, pl.ds(start, step_rows)].astype(jnp.float32)
            row = start + lax.broadcasted_iota(jnp.int32, shape, 0)
            in1 = (row >= lag) & (row < lag + SPAN)
            total0 += jnp.sum(jnp.where(row < SPAN, values, 0.0), 0, keepdims=True)
            total1 += jnp.sum(jnp.where(in1, values, 0.0), 0, keepdims=True)
            return total0, total1

        total0, total1 = lax.fori_loop(0, WINDOW // step_rows, add, (zero, zero))
        sums[group, h] = jnp.concatenate(
            [total0, total1, jnp.zeros((6, chunk_width), jnp.float32)], 0
        )

    def spread(buf, ssem, rsem):
        copies = []
        for d in range(1, nf):
            copy = remote(
                buf.at[group], buf.at[group], ssem.at[d], rsem.at[d],
                {"frames": (group + d) % nf},
            )
            copy.start()
            copies.append(copy)
        return copies

    sum_copies = spread(sums, sum_send, sum_recv)
    pass_across(0)
    forward(0, 1)
    for copy in sum_copies:
        copy.wait()
    means = (sums[0] + sums[1] + sums[2] + sums[3]) / (nf * SPAN)
    for h in range(CHUNKS):
        mean0 = means[h, 0:1]

        def add_squares(i, total, h=h, mean0=mean0):
            start = pl.multiple_of(i * step_rows, step_rows)
            values = raw_ref[h, pl.ds(start, step_rows)].astype(jnp.float32)
            cent = (values - mean0).astype(jnp.bfloat16).astype(jnp.float32)
            return total + jnp.sum(cent * cent, 0, keepdims=True)

        total = lax.fori_loop(0, SPAN // step_rows, add_squares, zero)
        squares[group, h] = jnp.broadcast_to(total, (8, chunk_width))
    sq_copies = spread(squares, sq_send, sq_recv)
    forward(0, 2)
    if CHUNKS > 1:
        start_own(1)
    for copy in sq_copies:
        copy.wait()
    total = squares[0] + squares[1] + squares[2] + squares[3]
    kind = lax.broadcasted_iota(jnp.int32, total.shape, 1)
    stats_ref[me] = jnp.where(kind < 2, means, total)
    st_copies = []
    for d in range(1, nb):
        copy = remote(
            stats_ref.at[me], stats_ref.at[me], st_send.at[d], st_recv.at[d],
            {"blocks": (me + d) % nb},
        )
        copy.start()
        st_copies.append(copy)
    source = lax.broadcasted_iota(jnp.int32, (SPAN, WINDOW), 1)
    target = lax.broadcasted_iota(jnp.int32, (SPAN, WINDOW), 0)
    shift[...] = jnp.where(source == target + lag, 1.0, 0.0).astype(jnp.bfloat16)
    for dist in range(3, nz):
        forward(0, dist)
    rest(0)
    for copy in st_copies + own:
        copy.wait()

    split = maxown // 2
    for h in range(1, CHUNKS):
        pass_across(h)
        forward(h, 1)
        if h >= 2:
            drain(h - 2)
        compute(h - 1, 0, split)
        forward(h, 2)
        if h + 1 < CHUNKS:
            start_own(h + 1)
        compute(h - 1, split, maxown + 1)
        for dist in range(3, nz):
            forward(h, dist)
        rest(h)
    if CHUNKS > 1:
        drain(CHUNKS - 2)
    compute(CHUNKS - 1, 0, maxown + 1)

    def finish(t, carry):
        for p in range(CHUNKS):
            y_copy(p, t).wait_recv()
        out_ref[t] += y_recv[t].astype(jnp.float32)
        return carry

    lax.fori_loop(0, 2 * maxown, finish, 0)
    drain(CHUNKS - 1)
    for cond, end in pending:
        if cond is None:
            end()
        else:
            pl.when(cond)(end)


def fused(raw, lag, table, maxown):
    nf = lax.axis_size("frames")
    nb = lax.axis_size("blocks")
    width = raw.shape[2]
    rows = width // 4
    n, most, every = 2 * maxown, 2 * CHUNKS - 1, CHUNKS * CHUNKS
    pieces = len(ZX_PIECES) + 1
    dma = pltpu.SemaphoreType.DMA
    smem = pl.BlockSpec(memory_space=pltpu.SMEM)
    vmem = pl.BlockSpec(memory_space=pltpu.VMEM)
    bf16, f32 = jnp.bfloat16, jnp.float32
    return pl.pallas_call(
        functools.partial(fused_kernel, nb // 2, maxown),
        out_shape=(
            jax.ShapeDtypeStruct((n, every, rows, width), f32),
            jax.ShapeDtypeStruct((nb, CHUNKS, 8, width), f32),
        ),
        in_specs=[smem, smem, vmem],
        out_specs=(vmem, vmem),
        scratch_shapes=[
            pltpu.VMEM((nf, CHUNKS, 8, width), f32),
            pltpu.VMEM((nf, CHUNKS, 8, width), f32),
            pltpu.VMEM((SPAN, WINDOW), bf16),
            pltpu.VMEM((CHUNKS, 2 * SPAN, width), bf16),
            pltpu.VMEM((CHUNKS, 2 * SPAN, width), bf16),
            pltpu.VMEM((width, width), f32),
            pltpu.VMEM((4, 2, most, rows, width), bf16),
            pltpu.VMEM((n, 2, every, rows, width), bf16),
            pltpu.VMEM((4, most, rows, width), f32),
            pltpu.VMEM((n, most, rows, width), bf16),
            pltpu.VMEM((n, every, rows, width), bf16),
            dma((3, nb, CHUNKS, pieces)),
            dma((nb, CHUNKS, pieces)),
            dma((CHUNKS,)),
            dma((nf,)),
            dma((nf,)),
            dma((nf,)),
            dma((nf,)),
            dma((nb,)),
            dma((nb,)),
            dma((4, 2)),
            dma((CHUNKS, n, 2)),
            dma((n,)),
            dma((CHUNKS, n)),
        ]
        + [pltpu.VMEM((nb, WINDOW, width), bf16)] * CHUNKS,
        compiler_params=pltpu.CompilerParams(
            collective_id=0, has_side_effects=True, vmem_limit_bytes=61 * 2**20
        ),
        name="fused",
    )(lag, table, raw)


def products_kernel(
    maxown, table_ref, full0_ref, full1_ref, out_ref,
    core_send, core_recv, held, y_send, y_recv,
    cs_sem, cr_sem, ys_sem, yr_sem,
):
    group = lax.axis_index("frames")
    y, core = group // 2, group % 2
    mate = y * 2 + 1 - core
    far = (1 - y) * 2 + core
    quarter = BS // 4
    barrier = pltpu.get_barrier_semaphore()
    for other in (mate, far):
        pl.semaphore_signal(barrier, inc=1, device_id={"frames": other}, device_id_type=MESH)
    pl.semaphore_wait(barrier, 2)
    contract = (((0,), (0,)), ((), ()))

    def dot(a, b):
        return lax.dot_general(a, b, contract, preferred_element_type=jnp.float32)

    def core_copy(t, part):
        return remote(
            core_send.at[t % 4, part], core_recv.at[t, part],
            cs_sem.at[t % 4, part], cr_sem.at[t, part], {"frames": mate},
        )

    def y_copy(t):
        return remote(
            y_send.at[t % 4], y_recv.at[t], ys_sem.at[t % 4], yr_sem.at[t], {"frames": far}
        )

    def multiply(s):
        i = table_ref[0, s]
        j = table_ref[1, s]

        def part(row_quarter, store):
            cols = pl.ds(pl.multiple_of(row_quarter * quarter, quarter), quarter)
            left0 = full0_ref[i, :, cols]
            left1 = full1_ref[i, :, cols]
            store(0, dot(left0, full0_ref[j]))
            store(1, dot(left0, full1_ref[j]) + dot(left1, full0_ref[j]))

        for p, row_quarter in enumerate(((1 - y) * 2 + 1 - core, y * 2 + 1 - core)):
            def to_mate(o, value, p=p):
                t = s * 2 + o

                @pl.when(s >= 2)
                def _():
                    core_copy(t, p).wait_send()

                core_send[t % 4, p] = value.astype(jnp.bfloat16)
                core_copy(t, p).start()

            part(row_quarter, to_mate)

        def keep_far(o, value):
            held[(s % 2) * 2 + o] = value

        def keep_mine(o, value):
            out_ref[s * 2 + o] = value

        part((1 - y) * 2 + core, keep_far)
        part(y * 2 + core, keep_mine)

    def pass_on(s):
        for o in range(2):
            t = s * 2 + o
            core_copy(t, 0).wait_recv()
            core_copy(t, 1).wait_recv()

            @pl.when(s >= 2)
            def _():
                y_copy(t).wait_send()

            y_send[t % 4] = (
                held[(s % 2) * 2 + o] + core_recv[t, 0].astype(jnp.float32)
            ).astype(jnp.bfloat16)
            y_copy(t).start()
            out_ref[t] += core_recv[t, 1].astype(jnp.float32)

    def step(s, carry):
        pl.when(s < maxown)(lambda: multiply(s))
        pl.when(s >= 1)(lambda: pass_on(s - 1))
        return carry

    lax.fori_loop(0, maxown + 1, step, 0)

    def finish(t, carry):
        y_copy(t).wait_recv()
        out_ref[t] += y_recv[t].astype(jnp.float32)
        return carry

    lax.fori_loop(0, 2 * maxown, finish, 0)
    for t in range(max(0, 2 * maxown - 4), 2 * maxown):
        y_copy(t).wait_send()
        core_copy(t, 0).wait_send()
        core_copy(t, 1).wait_send()


def owned_products(table, full0, full1, maxown):
    quarter = BS // 4
    n = 2 * maxown
    dma = pltpu.SemaphoreType.DMA
    vmem = pl.BlockSpec(memory_space=pltpu.VMEM)
    return pl.pallas_call(
        functools.partial(products_kernel, maxown),
        out_shape=jax.ShapeDtypeStruct((n, quarter, BS), jnp.float32),
        in_specs=[pl.BlockSpec(memory_space=pltpu.SMEM), vmem, vmem],
        out_specs=vmem,
        scratch_shapes=[
            pltpu.VMEM((4, 2, quarter, BS), jnp.bfloat16),
            pltpu.VMEM((n, 2, quarter, BS), jnp.bfloat16),
            pltpu.VMEM((4, quarter, BS), jnp.float32),
            pltpu.VMEM((4, quarter, BS), jnp.bfloat16),
            pltpu.VMEM((n, quarter, BS), jnp.bfloat16),
            dma((4, 2)),
            dma((n, 2)),
            dma((4,)),
            dma((n,)),
        ],
        compiler_params=pltpu.CompilerParams(
            collective_id=1, has_side_effects=True, vmem_limit_bytes=60 * 2**20
        ),
        name="owned_products",
    )(table, full0, full1)


def gather_plain(raw, lag):
    nframes = lax.axis_size("frames")
    count = nframes * SPAN
    first = raw[:SPAN].astype(jnp.float32)
    later = lax.dynamic_slice_in_dim(raw, lag, SPAN, 0).astype(jnp.float32)
    means = lax.psum(jnp.stack([jnp.sum(first, 0), jnp.sum(later, 0)]), "frames") / count
    cent0 = (first - means[0]).astype(jnp.bfloat16)
    own = lax.psum(jnp.sum(jnp.square(cent0.astype(jnp.float32)), 0), "frames")
    stats = jnp.concatenate([means, own[None]], 0)
    return lax.all_gather(raw, "blocks", axis=0), lax.all_gather(stats, "blocks", axis=0)


def shards(traj, span_offsets, lag, owner):
    nframes = lax.axis_size("frames")
    nblocks = lax.axis_size("blocks")
    group = lax.axis_index("frames")
    device = lax.axis_index("blocks")
    width = traj.shape[1] * nblocks
    nfeat = width // BS
    quarter = BS // nframes
    offset = jnp.sum(jnp.where(jnp.arange(nframes) == group, span_offsets, 0))
    raw = lax.dynamic_slice_in_dim(traj, offset, WINDOW, 0)

    rows_np, cols_np = np.triu_indices(nfeat)
    npairs = rows_np.shape[0]
    maxown = (npairs + nblocks - 1) // nblocks
    before = jnp.asarray(np.tril(np.ones((npairs, npairs), np.int32), -1))
    mine = owner == device
    rank = jnp.sum(before * mine.astype(jnp.int32)[None, :], 1)
    selected = mine[None, :] & (rank[None, :] == jnp.arange(maxown)[:, None])
    present = jnp.any(selected, 1)
    row_block = jnp.sum(jnp.where(selected, jnp.asarray(rows_np.astype(np.int32)), 0), 1)
    col_block = jnp.sum(jnp.where(selected, jnp.asarray(cols_np.astype(np.int32)), 0), 1)
    table = jnp.stack([row_block, col_block]).astype(jnp.int32)

    if nblocks == 8 and nframes == 4:
        lanes = quarter // CHUNKS
        raw = raw.reshape(WINDOW, 4, CHUNKS, lanes).transpose(2, 0, 1, 3)
        total, stats = fused(raw.reshape(CHUNKS, WINDOW, 4 * lanes), lag, table, maxown)
        squares = stats[:, :, 2].reshape(nfeat, CHUNKS, 4, lanes)
        squares = squares.transpose(0, 2, 1, 3).reshape(nfeat, BS)
        order = shells()
        order = [order.index((r, c)) for r in range(CHUNKS) for c in range(CHUNKS)]
        total = jnp.stack([total[:, k] for k in order], 1)
        total = total.reshape(maxown, 2, CHUNKS, CHUNKS, lanes, 4, lanes)
        total = total.transpose(0, 1, 2, 4, 5, 3, 6)
    else:
        gathered, stats = gather_plain(raw, lag[0])
        split = (nfeat, nblocks // nfeat)
        gathered = gathered.reshape(split + gathered.shape[1:])
        gathered = jnp.swapaxes(gathered, 1, 2).reshape(nfeat, WINDOW, BS)
        stats = stats.reshape(split + stats.shape[1:])
        stats = jnp.swapaxes(stats, 1, 2).reshape(nfeat, stats.shape[2], BS)
        full0 = (gathered[:, :SPAN].astype(jnp.float32) - stats[:, 0:1]).astype(jnp.bfloat16)
        full1 = lax.dynamic_slice_in_dim(gathered, lag[0], SPAN, 1).astype(jnp.float32)
        full1 = (full1 - stats[:, 1:2]).astype(jnp.bfloat16)
        squares = stats[:, 2]
        total = owned_products(table, full0, full1, maxown)
    inv = 1.0 / jnp.sqrt(squares + eps)
    total = total.reshape(maxown, 2, quarter, BS)
    mine_inv = lax.dynamic_slice_in_dim(inv, group * quarter, quarter, 1)
    row_inv = jnp.where(present[:, None], jnp.take(mine_inv, row_block, axis=0), 0.0)
    col_inv = jnp.take(inv, col_block, axis=0)
    corr_inst = total[:, 0] * row_inv[:, :, None] * col_inv[:, None, :]
    corr_lag = 0.5 * total[:, 1] * row_inv[:, :, None] * col_inv[:, None, :]
    return (corr_inst.astype(jnp.bfloat16), corr_lag.astype(jnp.bfloat16))


def solution(mesh):
    in_specs = (P("frames", "blocks"), P(), P(), P())
    out_specs = (P("blocks", "frames", None), P("blocks", "frames", None))
    return jax.shard_map(shards, mesh=mesh, in_specs=in_specs, out_specs=out_specs, check_vma=False)
```

```python
import functools

import jax
import jax.numpy as jnp
import numpy as np
from jax import lax
from jax.experimental import pallas as pl
from jax.experimental.pallas import tpu as pltpu
from jax.sharding import PartitionSpec as P

BS = 1024
SPAN = 512
MAXLAG = 256
WINDOW = SPAN + MAXLAG
CHUNKS = 2
ZX_PIECES = ((0, 320), (320, 320))
XZ_PIECE = (640, 128)
eps = 1e-06
MESH = pl.DeviceIdType.MESH


def remote(src, dst, send_sem, recv_sem, device_id):
    return pltpu.make_async_remote_copy(
        src_ref=src,
        dst_ref=dst,
        send_sem=send_sem,
        recv_sem=recv_sem,
        device_id=device_id,
        device_id_type=MESH,
    )


def shells():
    tiles = []
    for p in range(CHUNKS):
        tiles += [(p, c) for c in range(p + 1)] + [(r, p) for r in range(p)]
    return tiles


def fused_kernel(
    nz, maxown, lag_ref, table_ref, raw_ref, out_ref, stats_ref,
    sums, squares, shift, left, right, prod,
    core_send, core_recv, held, y_send, y_recv,
    send_sem, recv_sem, own_sem,
    sum_send, sum_recv, sq_send, sq_recv, st_send, st_recv,
    cs_sem, cr_sem, ys_sem, yr_sem, *gat,
):
    nf = lax.axis_size("frames")
    nb = 2 * nz
    group = lax.axis_index("frames")
    me = lax.axis_index("blocks")
    z, x = me // 2, me % 2
    y, core = group // 2, group % 2
    mate = y * 2 + 1 - core
    far = (1 - y) * 2 + core
    across = z * 2 + 1 - x
    chunk_width = raw_ref.shape[2]
    rows = chunk_width // 4

    barrier = pltpu.get_barrier_semaphore()
    for d in range(1, nb):
        pl.semaphore_signal(
            barrier, inc=1, device_id={"blocks": (me + d) % nb}, device_id_type=MESH
        )
    for d in range(1, nf):
        pl.semaphore_signal(
            barrier, inc=1, device_id={"frames": (group + d) % nf}, device_id_type=MESH
        )
    pl.semaphore_wait(barrier, nb + nf - 2)

    pending = []
    last = len(ZX_PIECES)
    pieces = ZX_PIECES + (XZ_PIECE,)

    def send(cond, h, block, k, way, target):
        start, size = pieces[k]
        span = pl.ds(start, size)
        src = raw_ref.at[h, span] if block is me else gat[h].at[block, span]

        def copy():
            return remote(
                src,
                gat[h].at[block, span],
                send_sem.at[way, block, h, k],
                recv_sem.at[block, h, k],
                {"blocks": target},
            )

        def go():
            copy().start()

        def end():
            copy().wait_send()

        if cond is None:
            go()
        else:
            pl.when(cond)(go)
        pending.append((cond, end))

    def arrived(h, block, k):
        start, size = pieces[k]
        here = gat[h].at[block, pl.ds(start, size)]
        pltpu.make_async_copy(here, here, recv_sem.at[block, h, k]).wait()

    up, down = me + 2, me - 2
    is_up, is_down = z < nz - 1, z > 0

    def start_own(h):
        send(None, h, me, last, 2, across)
        for k in range(last + 1):
            send(is_up, h, me, k, 0, up)
            send(is_down, h, me, k, 1, down)
            if k < last:
                send(None, h, me, k, 2, across)

    def pass_across(h):
        arrived(h, across, last)
        send(is_up, h, across, last, 0, up)
        send(is_down, h, across, last, 1, down)

    def forward(h, dist):
        for k in range(last):
            for side in (-1, 1):
                zb = z + side * dist
                have = (zb >= 0) if side < 0 else (zb < nz)
                block = zb * 2 + x
                on = have & (is_up if side < 0 else is_down)
                pl.when(have)(functools.partial(arrived, h, block, k))
                send(on, h, block, k, 0 if side < 0 else 1, up if side < 0 else down)
                send(have, h, block, k, 2, across)
        for side in (-1, 1):
            zb = z + side * dist
            have = (zb >= 0) if side < 0 else (zb < nz)
            on = have & (is_up if side < 0 else is_down)
            for block in (zb * 2 + x, zb * 2 + 1 - x):
                pl.when(have)(functools.partial(arrived, h, block, last))
                send(on, h, block, last, 0 if side < 0 else 1, up if side < 0 else down)

    def rest(h):
        for k in range(last):
            arrived(h, across, k)
        for dist in range(1, nz):
            for side in (-1, 1):
                zb = z + side * dist
                have = (zb >= 0) if side < 0 else (zb < nz)
                for k in range(last):
                    pl.when(have)(functools.partial(arrived, h, zb * 2 + 1 - x, k))

    def core_copy(p, t, part):
        n = 2 * p + 1
        return remote(
            core_send.at[t % 4, part, pl.ds(0, n)],
            core_recv.at[t, part, pl.ds(p * p, n)],
            cs_sem.at[t % 4, part], cr_sem.at[p, t, part], {"frames": mate},
        )

    def y_copy(p, t):
        n = 2 * p + 1
        return remote(
            y_send.at[t, pl.ds(0, n)], y_recv.at[t, pl.ds(p * p, n)],
            ys_sem.at[t], yr_sem.at[p, t], {"frames": far},
        )

    tiles = shells()
    contract = (((0,), (0,)), ((), ()))

    def dot(a, b):
        return lax.dot_general(a, b, contract, preferred_element_type=jnp.float32)

    def center(block, h, target, first, second):
        base = gat[h][block, pl.ds(0, SPAN)].astype(jnp.float32)
        target[h, pl.ds(first, SPAN)] = (base - stats_ref[block, h, 0:1]).astype(jnp.bfloat16)
        later = jnp.dot(shift[...], gat[h][block], preferred_element_type=jnp.float32)
        target[h, pl.ds(second, SPAN)] = (later - stats_ref[block, h, 1:2]).astype(jnp.bfloat16)

    def place(t, tile, value, add):
        r, c = tiles[tile]
        for q in range(4):
            where = (t, pl.ds(r * rows, rows), pl.ds((q * CHUNKS + c) * rows, rows))
            part = value[:, q * rows : (q + 1) * rows]
            out_ref[where] = out_ref[where] + part if add else part

    def multiply(p, s):
        i = table_ref[0, s]
        j = table_ref[1, s]
        for h in range(p + 1):
            center(i, h, left, 0, SPAN)
            center(j, h, right, SPAN, 0)

        @pl.when(s >= 2)
        def _():
            for o in range(2):
                for part in range(2):
                    core_copy(p, s * 2 + o, part).wait_send()

        for o in range(2):
            t = s * 2 + o
            for n in range(2 * p + 1):
                r, c = tiles[p * p + n]
                if o == 0:
                    prod[...] = dot(left[r, 0:SPAN], right[c, SPAN : 2 * SPAN])
                else:
                    prod[...] = dot(left[r], right[c])

                def quarter(q):
                    return prod[pl.ds(pl.multiple_of(q * rows, rows), rows)]

                core_send[t % 4, 0, n] = quarter((1 - y) * 2 + 1 - core).astype(jnp.bfloat16)
                core_send[t % 4, 1, n] = quarter(y * 2 + 1 - core).astype(jnp.bfloat16)
                held[t % 4, n] = quarter((1 - y) * 2 + core)
                place(t, p * p + n, quarter(y * 2 + core), False)
            core_copy(p, t, 0).start()
            core_copy(p, t, 1).start()

    def pass_on(p, s):
        span = pl.ds(p * p, 2 * p + 1)
        for o in range(2):
            t = s * 2 + o
            core_copy(p, t, 0).wait_recv()
            core_copy(p, t, 1).wait_recv()
            y_send[t, pl.ds(0, 2 * p + 1)] = (
                held[t % 4, pl.ds(0, 2 * p + 1)] + core_recv[t, 0, span].astype(jnp.float32)
            ).astype(jnp.bfloat16)
            y_copy(p, t).start()
            for tile in range(p * p, (p + 1) * (p + 1)):
                place(t, tile, core_recv[t, 1, tile].astype(jnp.float32), True)

    def compute(p, low, high):
        def step(s, carry):
            pl.when(s < maxown)(lambda: multiply(p, s))
            pl.when(s >= 1)(lambda: pass_on(p, s - 1))
            return carry

        lax.fori_loop(low, high, step, 0)

    def drain(p):
        for t in range(max(0, 2 * maxown - 4), 2 * maxown):
            core_copy(p, t, 0).wait_send()
            core_copy(p, t, 1).wait_send()
        for t in range(2 * maxown):
            y_copy(p, t).wait_send()

    start_own(0)
    own = [
        pltpu.make_async_copy(raw_ref.at[h], gat[h].at[me], own_sem.at[h]) for h in range(CHUNKS)
    ]
    for copy in own:
        copy.start()
    lag = lag_ref[0]
    step_rows = 64
    shape = (step_rows, chunk_width)
    zero = jnp.zeros((1, chunk_width), jnp.float32)
    for h in range(CHUNKS):

        def add(i, carry, h=h):
            total0, total1 = carry
            start = pl.multiple_of(i * step_rows, step_rows)
            values = raw_ref[h, pl.ds(start, step_rows)].astype(jnp.float32)
            row = start + lax.broadcasted_iota(jnp.int32, shape, 0)
            in1 = (row >= lag) & (row < lag + SPAN)
            total0 += jnp.sum(jnp.where(row < SPAN, values, 0.0), 0, keepdims=True)
            total1 += jnp.sum(jnp.where(in1, values, 0.0), 0, keepdims=True)
            return total0, total1

        total0, total1 = lax.fori_loop(0, WINDOW // step_rows, add, (zero, zero))
        sums[group, h] = jnp.concatenate(
            [total0, total1, jnp.zeros((6, chunk_width), jnp.float32)], 0
        )

    def spread(buf, ssem, rsem):
        copies = []
        for d in range(1, nf):
            copy = remote(
                buf.at[group], buf.at[group], ssem.at[d], rsem.at[d],
                {"frames": (group + d) % nf},
            )
            copy.start()
            copies.append(copy)
        return copies

    sum_copies = spread(sums, sum_send, sum_recv)
    pass_across(0)
    forward(0, 1)
    for copy in sum_copies:
        copy.wait()
    means = (sums[0] + sums[1] + sums[2] + sums[3]) / (nf * SPAN)
    for h in range(CHUNKS):
        mean0 = means[h, 0:1]

        def add_squares(i, total, h=h, mean0=mean0):
            start = pl.multiple_of(i * step_rows, step_rows)
            values = raw_ref[h, pl.ds(start, step_rows)].astype(jnp.float32)
            cent = (values - mean0).astype(jnp.bfloat16).astype(jnp.float32)
            return total + jnp.sum(cent * cent, 0, keepdims=True)

        total = lax.fori_loop(0, SPAN // step_rows, add_squares, zero)
        squares[group, h] = jnp.broadcast_to(total, (8, chunk_width))
    sq_copies = spread(squares, sq_send, sq_recv)
    forward(0, 2)
    if CHUNKS > 1:
        start_own(1)
    for copy in sq_copies:
        copy.wait()
    total = squares[0] + squares[1] + squares[2] + squares[3]
    kind = lax.broadcasted_iota(jnp.int32, total.shape, 1)
    stats_ref[me] = jnp.where(kind < 2, means, total)
    st_copies = []
    for d in range(1, nb):
        copy = remote(
            stats_ref.at[me], stats_ref.at[me], st_send.at[d], st_recv.at[d],
            {"blocks": (me + d) % nb},
        )
        copy.start()
        st_copies.append(copy)
    source = lax.broadcasted_iota(jnp.int32, (SPAN, WINDOW), 1)
    target = lax.broadcasted_iota(jnp.int32, (SPAN, WINDOW), 0)
    shift[...] = jnp.where(source == target + lag, 1.0, 0.0).astype(jnp.bfloat16)
    for dist in range(3, nz):
        forward(0, dist)
    rest(0)
    for copy in st_copies + own:
        copy.wait()

    split = maxown // 2
    for h in range(1, CHUNKS):
        pass_across(h)
        forward(h, 1)
        if h >= 2:
            drain(h - 2)
        compute(h - 1, 0, split)
        forward(h, 2)
        if h + 1 < CHUNKS:
            start_own(h + 1)
        compute(h - 1, split, maxown + 1)
        for dist in range(3, nz):
            forward(h, dist)
        rest(h)
    if CHUNKS > 1:
        drain(CHUNKS - 2)
    compute(CHUNKS - 1, 0, maxown + 1)

    def finish(t, carry):
        for p in range(CHUNKS):
            y_copy(p, t).wait_recv()
        for tile in range(CHUNKS * CHUNKS):
            place(t, tile, y_recv[t, tile].astype(jnp.float32), True)
        return carry

    lax.fori_loop(0, 2 * maxown, finish, 0)
    drain(CHUNKS - 1)
    for cond, end in pending:
        if cond is None:
            end()
        else:
            pl.when(cond)(end)


def fused(raw, lag, table, maxown):
    nf = lax.axis_size("frames")
    nb = lax.axis_size("blocks")
    width = raw.shape[2]
    rows = width // 4
    n, most, every = 2 * maxown, 2 * CHUNKS - 1, CHUNKS * CHUNKS
    pieces = len(ZX_PIECES) + 1
    dma = pltpu.SemaphoreType.DMA
    smem = pl.BlockSpec(memory_space=pltpu.SMEM)
    vmem = pl.BlockSpec(memory_space=pltpu.VMEM)
    bf16, f32 = jnp.bfloat16, jnp.float32
    return pl.pallas_call(
        functools.partial(fused_kernel, nb // 2, maxown),
        out_shape=(
            jax.ShapeDtypeStruct((n, CHUNKS * rows, CHUNKS * width), f32),
            jax.ShapeDtypeStruct((nb, CHUNKS, 8, width), f32),
        ),
        in_specs=[smem, smem, vmem],
        out_specs=(vmem, vmem),
        scratch_shapes=[
            pltpu.VMEM((nf, CHUNKS, 8, width), f32),
            pltpu.VMEM((nf, CHUNKS, 8, width), f32),
            pltpu.VMEM((SPAN, WINDOW), bf16),
            pltpu.VMEM((CHUNKS, 2 * SPAN, width), bf16),
            pltpu.VMEM((CHUNKS, 2 * SPAN, width), bf16),
            pltpu.VMEM((width, width), f32),
            pltpu.VMEM((4, 2, most, rows, width), bf16),
            pltpu.VMEM((n, 2, every, rows, width), bf16),
            pltpu.VMEM((4, most, rows, width), f32),
            pltpu.VMEM((n, most, rows, width), bf16),
            pltpu.VMEM((n, every, rows, width), bf16),
            dma((3, nb, CHUNKS, pieces)),
            dma((nb, CHUNKS, pieces)),
            dma((CHUNKS,)),
            dma((nf,)),
            dma((nf,)),
            dma((nf,)),
            dma((nf,)),
            dma((nb,)),
            dma((nb,)),
            dma((4, 2)),
            dma((CHUNKS, n, 2)),
            dma((n,)),
            dma((CHUNKS, n)),
        ]
        + [pltpu.VMEM((nb, WINDOW, width), bf16)] * CHUNKS,
        compiler_params=pltpu.CompilerParams(
            collective_id=0, has_side_effects=True, vmem_limit_bytes=61 * 2**20
        ),
        name="fused",
    )(lag, table, raw)


def products_kernel(
    maxown, table_ref, full0_ref, full1_ref, out_ref,
    core_send, core_recv, held, y_send, y_recv,
    cs_sem, cr_sem, ys_sem, yr_sem,
):
    group = lax.axis_index("frames")
    y, core = group // 2, group % 2
    mate = y * 2 + 1 - core
    far = (1 - y) * 2 + core
    quarter = BS // 4
    barrier = pltpu.get_barrier_semaphore()
    for other in (mate, far):
        pl.semaphore_signal(barrier, inc=1, device_id={"frames": other}, device_id_type=MESH)
    pl.semaphore_wait(barrier, 2)
    contract = (((0,), (0,)), ((), ()))

    def dot(a, b):
        return lax.dot_general(a, b, contract, preferred_element_type=jnp.float32)

    def core_copy(t, part):
        return remote(
            core_send.at[t % 4, part], core_recv.at[t, part],
            cs_sem.at[t % 4, part], cr_sem.at[t, part], {"frames": mate},
        )

    def y_copy(t):
        return remote(
            y_send.at[t % 4], y_recv.at[t], ys_sem.at[t % 4], yr_sem.at[t], {"frames": far}
        )

    def multiply(s):
        i = table_ref[0, s]
        j = table_ref[1, s]

        def part(row_quarter, store):
            cols = pl.ds(pl.multiple_of(row_quarter * quarter, quarter), quarter)
            left0 = full0_ref[i, :, cols]
            left1 = full1_ref[i, :, cols]
            store(0, dot(left0, full0_ref[j]))
            store(1, dot(left0, full1_ref[j]) + dot(left1, full0_ref[j]))

        for p, row_quarter in enumerate(((1 - y) * 2 + 1 - core, y * 2 + 1 - core)):
            def to_mate(o, value, p=p):
                t = s * 2 + o

                @pl.when(s >= 2)
                def _():
                    core_copy(t, p).wait_send()

                core_send[t % 4, p] = value.astype(jnp.bfloat16)
                core_copy(t, p).start()

            part(row_quarter, to_mate)

        def keep_far(o, value):
            held[(s % 2) * 2 + o] = value

        def keep_mine(o, value):
            out_ref[s * 2 + o] = value

        part((1 - y) * 2 + core, keep_far)
        part(y * 2 + core, keep_mine)

    def pass_on(s):
        for o in range(2):
            t = s * 2 + o
            core_copy(t, 0).wait_recv()
            core_copy(t, 1).wait_recv()

            @pl.when(s >= 2)
            def _():
                y_copy(t).wait_send()

            y_send[t % 4] = (
                held[(s % 2) * 2 + o] + core_recv[t, 0].astype(jnp.float32)
            ).astype(jnp.bfloat16)
            y_copy(t).start()
            out_ref[t] += core_recv[t, 1].astype(jnp.float32)

    def step(s, carry):
        pl.when(s < maxown)(lambda: multiply(s))
        pl.when(s >= 1)(lambda: pass_on(s - 1))
        return carry

    lax.fori_loop(0, maxown + 1, step, 0)

    def finish(t, carry):
        y_copy(t).wait_recv()
        out_ref[t] += y_recv[t].astype(jnp.float32)
        return carry

    lax.fori_loop(0, 2 * maxown, finish, 0)
    for t in range(max(0, 2 * maxown - 4), 2 * maxown):
        y_copy(t).wait_send()
        core_copy(t, 0).wait_send()
        core_copy(t, 1).wait_send()


def owned_products(table, full0, full1, maxown):
    quarter = BS // 4
    n = 2 * maxown
    dma = pltpu.SemaphoreType.DMA
    vmem = pl.BlockSpec(memory_space=pltpu.VMEM)
    return pl.pallas_call(
        functools.partial(products_kernel, maxown),
        out_shape=jax.ShapeDtypeStruct((n, quarter, BS), jnp.float32),
        in_specs=[pl.BlockSpec(memory_space=pltpu.SMEM), vmem, vmem],
        out_specs=vmem,
        scratch_shapes=[
            pltpu.VMEM((4, 2, quarter, BS), jnp.bfloat16),
            pltpu.VMEM((n, 2, quarter, BS), jnp.bfloat16),
            pltpu.VMEM((4, quarter, BS), jnp.float32),
            pltpu.VMEM((4, quarter, BS), jnp.bfloat16),
            pltpu.VMEM((n, quarter, BS), jnp.bfloat16),
            dma((4, 2)),
            dma((n, 2)),
            dma((4,)),
            dma((n,)),
        ],
        compiler_params=pltpu.CompilerParams(
            collective_id=1, has_side_effects=True, vmem_limit_bytes=60 * 2**20
        ),
        name="owned_products",
    )(table, full0, full1)


def gather_plain(raw, lag):
    nframes = lax.axis_size("frames")
    count = nframes * SPAN
    first = raw[:SPAN].astype(jnp.float32)
    later = lax.dynamic_slice_in_dim(raw, lag, SPAN, 0).astype(jnp.float32)
    means = lax.psum(jnp.stack([jnp.sum(first, 0), jnp.sum(later, 0)]), "frames") / count
    cent0 = (first - means[0]).astype(jnp.bfloat16)
    own = lax.psum(jnp.sum(jnp.square(cent0.astype(jnp.float32)), 0), "frames")
    stats = jnp.concatenate([means, own[None]], 0)
    return lax.all_gather(raw, "blocks", axis=0), lax.all_gather(stats, "blocks", axis=0)


def shards(traj, span_offsets, lag, owner):
    nframes = lax.axis_size("frames")
    nblocks = lax.axis_size("blocks")
    group = lax.axis_index("frames")
    device = lax.axis_index("blocks")
    width = traj.shape[1] * nblocks
    nfeat = width // BS
    quarter = BS // nframes
    offset = jnp.sum(jnp.where(jnp.arange(nframes) == group, span_offsets, 0))
    raw = lax.dynamic_slice_in_dim(traj, offset, WINDOW, 0)

    rows_np, cols_np = np.triu_indices(nfeat)
    npairs = rows_np.shape[0]
    maxown = (npairs + nblocks - 1) // nblocks
    before = jnp.asarray(np.tril(np.ones((npairs, npairs), np.int32), -1))
    mine = owner == device
    rank = jnp.sum(before * mine.astype(jnp.int32)[None, :], 1)
    selected = mine[None, :] & (rank[None, :] == jnp.arange(maxown)[:, None])
    present = jnp.any(selected, 1)
    row_block = jnp.sum(jnp.where(selected, jnp.asarray(rows_np.astype(np.int32)), 0), 1)
    col_block = jnp.sum(jnp.where(selected, jnp.asarray(cols_np.astype(np.int32)), 0), 1)
    table = jnp.stack([row_block, col_block]).astype(jnp.int32)

    if nblocks == 8 and nframes == 4:
        lanes = quarter // CHUNKS
        raw = [raw[:, k * lanes : (k + 1) * lanes] for k in range(4 * CHUNKS)]
        raw = jnp.stack([jnp.concatenate(raw[h::CHUNKS], 1) for h in range(CHUNKS)])
        total, stats = fused(raw, lag, table, maxown)
        squares = stats[:, :, 2].reshape(nfeat, CHUNKS, 4, lanes)
        squares = squares.transpose(0, 2, 1, 3).reshape(nfeat, BS)
    else:
        gathered, stats = gather_plain(raw, lag[0])
        split = (nfeat, nblocks // nfeat)
        gathered = gathered.reshape(split + gathered.shape[1:])
        gathered = jnp.swapaxes(gathered, 1, 2).reshape(nfeat, WINDOW, BS)
        stats = stats.reshape(split + stats.shape[1:])
        stats = jnp.swapaxes(stats, 1, 2).reshape(nfeat, stats.shape[2], BS)
        full0 = (gathered[:, :SPAN].astype(jnp.float32) - stats[:, 0:1]).astype(jnp.bfloat16)
        full1 = lax.dynamic_slice_in_dim(gathered, lag[0], SPAN, 1).astype(jnp.float32)
        full1 = (full1 - stats[:, 1:2]).astype(jnp.bfloat16)
        squares = stats[:, 2]
        total = owned_products(table, full0, full1, maxown)
    inv = 1.0 / jnp.sqrt(squares + eps)
    total = total.reshape(maxown, 2, quarter, BS)
    mine_inv = lax.dynamic_slice_in_dim(inv, group * quarter, quarter, 1)
    row_inv = jnp.where(present[:, None], jnp.take(mine_inv, row_block, axis=0), 0.0)
    col_inv = jnp.take(inv, col_block, axis=0)
    corr_inst = total[:, 0] * row_inv[:, :, None] * col_inv[:, None, :]
    corr_lag = 0.5 * total[:, 1] * row_inv[:, :, None] * col_inv[:, None, :]
    return (corr_inst.astype(jnp.bfloat16), corr_lag.astype(jnp.bfloat16))


def solution(mesh):
    in_specs = (P("frames", "blocks"), P(), P(), P())
    out_specs = (P("blocks", "frames", None), P("blocks", "frames", None))
    return jax.shard_map(shards, mesh=mesh, in_specs=in_specs, out_specs=out_specs, check_vma=False)
```

```python
import functools

import jax
import jax.numpy as jnp
import numpy as np
from jax import lax
from jax.experimental import pallas as pl
from jax.experimental.pallas import tpu as pltpu
from jax.sharding import PartitionSpec as P

BS = 1024
SPAN = 512
MAXLAG = 256
WINDOW = SPAN + MAXLAG
CHUNKS = 2
ZX_PIECES = ((0, 320), (320, 320))
XZ_PIECE = (640, 128)
eps = 1e-06
MESH = pl.DeviceIdType.MESH


def remote(src, dst, send_sem, recv_sem, device_id):
    return pltpu.make_async_remote_copy(
        src_ref=src,
        dst_ref=dst,
        send_sem=send_sem,
        recv_sem=recv_sem,
        device_id=device_id,
        device_id_type=MESH,
    )


def shells():
    tiles = []
    for p in range(CHUNKS):
        tiles += [(p, c) for c in range(p + 1)] + [(r, p) for r in range(p)]
    return tiles


def fused_kernel(
    nz, maxown, lag_ref, table_ref, raw_ref, out_ref, stats_ref,
    sums, squares, shift, left, right, prod,
    core_send, core_recv, held, y_send, y_recv,
    send_sem, recv_sem, own_sem,
    sum_send, sum_recv, sq_send, sq_recv, st_send, st_recv,
    cs_sem, cr_sem, ys_sem, yr_sem, *gat,
):
    nf = lax.axis_size("frames")
    nb = 2 * nz
    group = lax.axis_index("frames")
    me = lax.axis_index("blocks")
    z, x = me // 2, me % 2
    y, core = group // 2, group % 2
    mate = y * 2 + 1 - core
    far = (1 - y) * 2 + core
    across = z * 2 + 1 - x
    chunk_width = raw_ref.shape[2]
    rows = chunk_width // 4

    barrier = pltpu.get_barrier_semaphore()
    for d in range(1, nb):
        pl.semaphore_signal(
            barrier, inc=1, device_id={"blocks": (me + d) % nb}, device_id_type=MESH
        )
    for d in range(1, nf):
        pl.semaphore_signal(
            barrier, inc=1, device_id={"frames": (group + d) % nf}, device_id_type=MESH
        )
    pl.semaphore_wait(barrier, nb + nf - 2)

    pending = []
    last = len(ZX_PIECES)
    pieces = ZX_PIECES + (XZ_PIECE,)

    def send(cond, h, block, k, way, target):
        start, size = pieces[k]
        span = pl.ds(start, size)
        src = raw_ref.at[h, span] if block is me else gat[h].at[block, span]

        def copy():
            return remote(
                src,
                gat[h].at[block, span],
                send_sem.at[way, block, h, k],
                recv_sem.at[block, h, k],
                {"blocks": target},
            )

        def go():
            copy().start()

        def end():
            copy().wait_send()

        if cond is None:
            go()
        else:
            pl.when(cond)(go)
        pending.append((cond, end))

    def arrived(h, block, k):
        start, size = pieces[k]
        here = gat[h].at[block, pl.ds(start, size)]
        pltpu.make_async_copy(here, here, recv_sem.at[block, h, k]).wait()

    up, down = me + 2, me - 2
    is_up, is_down = z < nz - 1, z > 0

    def start_own(h):
        send(None, h, me, last, 2, across)
        for k in range(last + 1):
            send(is_up, h, me, k, 0, up)
            send(is_down, h, me, k, 1, down)
            if k < last:
                send(None, h, me, k, 2, across)

    def pass_across(h):
        arrived(h, across, last)
        send(is_up, h, across, last, 0, up)
        send(is_down, h, across, last, 1, down)

    def forward(h, dist):
        for k in range(last):
            for side in (-1, 1):
                zb = z + side * dist
                have = (zb >= 0) if side < 0 else (zb < nz)
                block = zb * 2 + x
                on = have & (is_up if side < 0 else is_down)
                pl.when(have)(functools.partial(arrived, h, block, k))
                send(on, h, block, k, 0 if side < 0 else 1, up if side < 0 else down)
                send(have, h, block, k, 2, across)
        for side in (-1, 1):
            zb = z + side * dist
            have = (zb >= 0) if side < 0 else (zb < nz)
            on = have & (is_up if side < 0 else is_down)
            for block in (zb * 2 + x, zb * 2 + 1 - x):
                pl.when(have)(functools.partial(arrived, h, block, last))
                send(on, h, block, last, 0 if side < 0 else 1, up if side < 0 else down)

    def rest(h):
        for k in range(last):
            arrived(h, across, k)
        for dist in range(1, nz):
            for side in (-1, 1):
                zb = z + side * dist
                have = (zb >= 0) if side < 0 else (zb < nz)
                for k in range(last):
                    pl.when(have)(functools.partial(arrived, h, zb * 2 + 1 - x, k))

    def core_copy(p, t, part):
        n = 2 * p + 1
        return remote(
            core_send.at[t % 4, part, pl.ds(0, n)],
            core_recv.at[t, part, pl.ds(p * p, n)],
            cs_sem.at[t % 4, part], cr_sem.at[p, t, part], {"frames": mate},
        )

    def y_copy(p, t):
        n = 2 * p + 1
        return remote(
            y_send.at[t, pl.ds(0, n)], y_recv.at[t, pl.ds(p * p, n)],
            ys_sem.at[t], yr_sem.at[p, t], {"frames": far},
        )

    tiles = shells()
    contract = (((0,), (0,)), ((), ()))

    def dot(a, b):
        return lax.dot_general(a, b, contract, preferred_element_type=jnp.float32)

    def center(block, h, target, first, second):
        base = gat[h][block, pl.ds(0, SPAN)].astype(jnp.float32)
        target[h, pl.ds(first, SPAN)] = (base - stats_ref[block, h, 0:1]).astype(jnp.bfloat16)
        later = jnp.dot(shift[...], gat[h][block], preferred_element_type=jnp.float32)
        target[h, pl.ds(second, SPAN)] = (later - stats_ref[block, h, 1:2]).astype(jnp.bfloat16)

    def place(t, tile, value, add):
        r, c = tiles[tile]
        for q in range(4):
            where = (t, pl.ds(r * rows, rows), pl.ds((q * CHUNKS + c) * rows, rows))
            part = value[:, q * rows : (q + 1) * rows]
            out_ref[where] = out_ref[where] + part if add else part

    def multiply(p, s):
        i = table_ref[0, s]
        j = table_ref[1, s]
        for h in range(p + 1):
            center(i, h, left, 0, SPAN)
            center(j, h, right, SPAN, 0)

        @pl.when(s >= 2)
        def _():
            for o in range(2):
                for part in range(2):
                    core_copy(p, s * 2 + o, part).wait_send()

        for o in range(2):
            t = s * 2 + o
            for n in range(2 * p + 1):
                r, c = tiles[p * p + n]
                if o == 0:
                    prod[...] = dot(left[r, 0:SPAN], right[c, SPAN : 2 * SPAN])
                else:
                    prod[...] = dot(left[r], right[c])

                def quarter(q):
                    return prod[pl.ds(pl.multiple_of(q * rows, rows), rows)]

                core_send[t % 4, 0, n] = quarter((1 - y) * 2 + 1 - core).astype(jnp.bfloat16)
                core_send[t % 4, 1, n] = quarter(y * 2 + 1 - core).astype(jnp.bfloat16)
                held[t % 4, n] = quarter((1 - y) * 2 + core)
                place(t, p * p + n, quarter(y * 2 + core), False)
            core_copy(p, t, 0).start()
            core_copy(p, t, 1).start()

    def pass_on(p, s):
        span = pl.ds(p * p, 2 * p + 1)
        for o in range(2):
            t = s * 2 + o
            core_copy(p, t, 0).wait_recv()
            core_copy(p, t, 1).wait_recv()
            y_send[t, pl.ds(0, 2 * p + 1)] = (
                held[t % 4, pl.ds(0, 2 * p + 1)] + core_recv[t, 0, span].astype(jnp.float32)
            ).astype(jnp.bfloat16)
            y_copy(p, t).start()
            for tile in range(p * p, (p + 1) * (p + 1)):
                place(t, tile, core_recv[t, 1, tile].astype(jnp.float32), True)

    def compute(p, low, high):
        def step(s, carry):
            pl.when(s < maxown)(lambda: multiply(p, s))
            pl.when(s >= 1)(lambda: pass_on(p, s - 1))
            return carry

        lax.fori_loop(low, high, step, 0)

    def drain(p):
        for t in range(max(0, 2 * maxown - 4), 2 * maxown):
            core_copy(p, t, 0).wait_send()
            core_copy(p, t, 1).wait_send()
        for t in range(2 * maxown):
            y_copy(p, t).wait_send()

    start_own(0)
    own = [
        pltpu.make_async_copy(raw_ref.at[h], gat[h].at[me], own_sem.at[h]) for h in range(CHUNKS)
    ]
    for copy in own:
        copy.start()
    lag = lag_ref[0]
    step_rows = 64
    shape = (step_rows, chunk_width)
    zero = jnp.zeros((1, chunk_width), jnp.float32)
    for h in range(CHUNKS):

        def add(i, carry, h=h):
            total0, total1 = carry
            start = pl.multiple_of(i * step_rows, step_rows)
            values = raw_ref[h, pl.ds(start, step_rows)].astype(jnp.float32)
            row = start + lax.broadcasted_iota(jnp.int32, shape, 0)
            in1 = (row >= lag) & (row < lag + SPAN)
            total0 += jnp.sum(jnp.where(row < SPAN, values, 0.0), 0, keepdims=True)
            total1 += jnp.sum(jnp.where(in1, values, 0.0), 0, keepdims=True)
            return total0, total1

        total0, total1 = lax.fori_loop(0, WINDOW // step_rows, add, (zero, zero))
        sums[group, h] = jnp.concatenate(
            [total0, total1, jnp.zeros((6, chunk_width), jnp.float32)], 0
        )

    def spread(buf, ssem, rsem):
        copies = []
        for d in range(1, nf):
            copy = remote(
                buf.at[group], buf.at[group], ssem.at[d], rsem.at[d],
                {"frames": (group + d) % nf},
            )
            copy.start()
            copies.append(copy)
        return copies

    sum_copies = spread(sums, sum_send, sum_recv)
    pass_across(0)
    forward(0, 1)
    if CHUNKS > 1:
        start_own(1)
    for copy in sum_copies:
        copy.wait()
    means = (sums[0] + sums[1] + sums[2] + sums[3]) / (nf * SPAN)
    for h in range(CHUNKS):
        mean0 = means[h, 0:1]

        def add_squares(i, total, h=h, mean0=mean0):
            start = pl.multiple_of(i * step_rows, step_rows)
            values = raw_ref[h, pl.ds(start, step_rows)].astype(jnp.float32)
            cent = (values - mean0).astype(jnp.bfloat16).astype(jnp.float32)
            return total + jnp.sum(cent * cent, 0, keepdims=True)

        total = lax.fori_loop(0, SPAN // step_rows, add_squares, zero)
        squares[group, h] = jnp.broadcast_to(total, (8, chunk_width))
    sq_copies = spread(squares, sq_send, sq_recv)
    forward(0, 2)
    for copy in sq_copies:
        copy.wait()
    total = squares[0] + squares[1] + squares[2] + squares[3]
    kind = lax.broadcasted_iota(jnp.int32, total.shape, 1)
    stats_ref[me] = jnp.where(kind < 2, means, total)
    st_copies = []
    for d in range(1, nb):
        copy = remote(
            stats_ref.at[me], stats_ref.at[me], st_send.at[d], st_recv.at[d],
            {"blocks": (me + d) % nb},
        )
        copy.start()
        st_copies.append(copy)
    source = lax.broadcasted_iota(jnp.int32, (SPAN, WINDOW), 1)
    target = lax.broadcasted_iota(jnp.int32, (SPAN, WINDOW), 0)
    shift[...] = jnp.where(source == target + lag, 1.0, 0.0).astype(jnp.bfloat16)
    for dist in range(3, nz):
        forward(0, dist)
    rest(0)
    for copy in st_copies + own:
        copy.wait()

    split = maxown // 2
    for h in range(1, CHUNKS):
        pass_across(h)
        forward(h, 1)
        if h >= 2:
            drain(h - 2)
        compute(h - 1, 0, split)
        forward(h, 2)
        if h + 1 < CHUNKS:
            start_own(h + 1)
        compute(h - 1, split, maxown + 1)
        for dist in range(3, nz):
            forward(h, dist)
        rest(h)
    if CHUNKS > 1:
        drain(CHUNKS - 2)
    compute(CHUNKS - 1, 0, maxown + 1)

    def finish(t, carry):
        for p in range(CHUNKS):
            y_copy(p, t).wait_recv()
        for tile in range(CHUNKS * CHUNKS):
            place(t, tile, y_recv[t, tile].astype(jnp.float32), True)
        return carry

    lax.fori_loop(0, 2 * maxown, finish, 0)
    drain(CHUNKS - 1)
    for cond, end in pending:
        if cond is None:
            end()
        else:
            pl.when(cond)(end)


def fused(raw, lag, table, maxown):
    nf = lax.axis_size("frames")
    nb = lax.axis_size("blocks")
    width = raw.shape[2]
    rows = width // 4
    n, most, every = 2 * maxown, 2 * CHUNKS - 1, CHUNKS * CHUNKS
    pieces = len(ZX_PIECES) + 1
    dma = pltpu.SemaphoreType.DMA
    smem = pl.BlockSpec(memory_space=pltpu.SMEM)
    vmem = pl.BlockSpec(memory_space=pltpu.VMEM)
    bf16, f32 = jnp.bfloat16, jnp.float32
    return pl.pallas_call(
        functools.partial(fused_kernel, nb // 2, maxown),
        out_shape=(
            jax.ShapeDtypeStruct((n, CHUNKS * rows, CHUNKS * width), f32),
            jax.ShapeDtypeStruct((nb, CHUNKS, 8, width), f32),
        ),
        in_specs=[smem, smem, vmem],
        out_specs=(vmem, vmem),
        scratch_shapes=[
            pltpu.VMEM((nf, CHUNKS, 8, width), f32),
            pltpu.VMEM((nf, CHUNKS, 8, width), f32),
            pltpu.VMEM((SPAN, WINDOW), bf16),
            pltpu.VMEM((CHUNKS, 2 * SPAN, width), bf16),
            pltpu.VMEM((CHUNKS, 2 * SPAN, width), bf16),
            pltpu.VMEM((width, width), f32),
            pltpu.VMEM((4, 2, most, rows, width), bf16),
            pltpu.VMEM((n, 2, every, rows, width), bf16),
            pltpu.VMEM((4, most, rows, width), f32),
            pltpu.VMEM((n, most, rows, width), bf16),
            pltpu.VMEM((n, every, rows, width), bf16),
            dma((3, nb, CHUNKS, pieces)),
            dma((nb, CHUNKS, pieces)),
            dma((CHUNKS,)),
            dma((nf,)),
            dma((nf,)),
            dma((nf,)),
            dma((nf,)),
            dma((nb,)),
            dma((nb,)),
            dma((4, 2)),
            dma((CHUNKS, n, 2)),
            dma((n,)),
            dma((CHUNKS, n)),
        ]
        + [pltpu.VMEM((nb, WINDOW, width), bf16)] * CHUNKS,
        compiler_params=pltpu.CompilerParams(
            collective_id=0, has_side_effects=True, vmem_limit_bytes=61 * 2**20
        ),
        name="fused",
    )(lag, table, raw)


def products_kernel(
    maxown, table_ref, full0_ref, full1_ref, out_ref,
    core_send, core_recv, held, y_send, y_recv,
    cs_sem, cr_sem, ys_sem, yr_sem,
):
    group = lax.axis_index("frames")
    y, core = group // 2, group % 2
    mate = y * 2 + 1 - core
    far = (1 - y) * 2 + core
    quarter = BS // 4
    barrier = pltpu.get_barrier_semaphore()
    for other in (mate, far):
        pl.semaphore_signal(barrier, inc=1, device_id={"frames": other}, device_id_type=MESH)
    pl.semaphore_wait(barrier, 2)
    contract = (((0,), (0,)), ((), ()))

    def dot(a, b):
        return lax.dot_general(a, b, contract, preferred_element_type=jnp.float32)

    def core_copy(t, part):
        return remote(
            core_send.at[t % 4, part], core_recv.at[t, part],
            cs_sem.at[t % 4, part], cr_sem.at[t, part], {"frames": mate},
        )

    def y_copy(t):
        return remote(
            y_send.at[t % 4], y_recv.at[t], ys_sem.at[t % 4], yr_sem.at[t], {"frames": far}
        )

    def multiply(s):
        i = table_ref[0, s]
        j = table_ref[1, s]

        def part(row_quarter, store):
            cols = pl.ds(pl.multiple_of(row_quarter * quarter, quarter), quarter)
            left0 = full0_ref[i, :, cols]
            left1 = full1_ref[i, :, cols]
            store(0, dot(left0, full0_ref[j]))
            store(1, dot(left0, full1_ref[j]) + dot(left1, full0_ref[j]))

        for p, row_quarter in enumerate(((1 - y) * 2 + 1 - core, y * 2 + 1 - core)):
            def to_mate(o, value, p=p):
                t = s * 2 + o

                @pl.when(s >= 2)
                def _():
                    core_copy(t, p).wait_send()

                core_send[t % 4, p] = value.astype(jnp.bfloat16)
                core_copy(t, p).start()

            part(row_quarter, to_mate)

        def keep_far(o, value):
            held[(s % 2) * 2 + o] = value

        def keep_mine(o, value):
            out_ref[s * 2 + o] = value

        part((1 - y) * 2 + core, keep_far)
        part(y * 2 + core, keep_mine)

    def pass_on(s):
        for o in range(2):
            t = s * 2 + o
            core_copy(t, 0).wait_recv()
            core_copy(t, 1).wait_recv()

            @pl.when(s >= 2)
            def _():
                y_copy(t).wait_send()

            y_send[t % 4] = (
                held[(s % 2) * 2 + o] + core_recv[t, 0].astype(jnp.float32)
            ).astype(jnp.bfloat16)
            y_copy(t).start()
            out_ref[t] += core_recv[t, 1].astype(jnp.float32)

    def step(s, carry):
        pl.when(s < maxown)(lambda: multiply(s))
        pl.when(s >= 1)(lambda: pass_on(s - 1))
        return carry

    lax.fori_loop(0, maxown + 1, step, 0)

    def finish(t, carry):
        y_copy(t).wait_recv()
        out_ref[t] += y_recv[t].astype(jnp.float32)
        return carry

    lax.fori_loop(0, 2 * maxown, finish, 0)
    for t in range(max(0, 2 * maxown - 4), 2 * maxown):
        y_copy(t).wait_send()
        core_copy(t, 0).wait_send()
        core_copy(t, 1).wait_send()


def owned_products(table, full0, full1, maxown):
    quarter = BS // 4
    n = 2 * maxown
    dma = pltpu.SemaphoreType.DMA
    vmem = pl.BlockSpec(memory_space=pltpu.VMEM)
    return pl.pallas_call(
        functools.partial(products_kernel, maxown),
        out_shape=jax.ShapeDtypeStruct((n, quarter, BS), jnp.float32),
        in_specs=[pl.BlockSpec(memory_space=pltpu.SMEM), vmem, vmem],
        out_specs=vmem,
        scratch_shapes=[
            pltpu.VMEM((4, 2, quarter, BS), jnp.bfloat16),
            pltpu.VMEM((n, 2, quarter, BS), jnp.bfloat16),
            pltpu.VMEM((4, quarter, BS), jnp.float32),
            pltpu.VMEM((4, quarter, BS), jnp.bfloat16),
            pltpu.VMEM((n, quarter, BS), jnp.bfloat16),
            dma((4, 2)),
            dma((n, 2)),
            dma((4,)),
            dma((n,)),
        ],
        compiler_params=pltpu.CompilerParams(
            collective_id=1, has_side_effects=True, vmem_limit_bytes=60 * 2**20
        ),
        name="owned_products",
    )(table, full0, full1)


def gather_plain(raw, lag):
    nframes = lax.axis_size("frames")
    count = nframes * SPAN
    first = raw[:SPAN].astype(jnp.float32)
    later = lax.dynamic_slice_in_dim(raw, lag, SPAN, 0).astype(jnp.float32)
    means = lax.psum(jnp.stack([jnp.sum(first, 0), jnp.sum(later, 0)]), "frames") / count
    cent0 = (first - means[0]).astype(jnp.bfloat16)
    own = lax.psum(jnp.sum(jnp.square(cent0.astype(jnp.float32)), 0), "frames")
    stats = jnp.concatenate([means, own[None]], 0)
    return lax.all_gather(raw, "blocks", axis=0), lax.all_gather(stats, "blocks", axis=0)


def shards(traj, span_offsets, lag, owner):
    nframes = lax.axis_size("frames")
    nblocks = lax.axis_size("blocks")
    group = lax.axis_index("frames")
    device = lax.axis_index("blocks")
    width = traj.shape[1] * nblocks
    nfeat = width // BS
    quarter = BS // nframes
    offset = jnp.sum(jnp.where(jnp.arange(nframes) == group, span_offsets, 0))
    raw = lax.dynamic_slice_in_dim(traj, offset, WINDOW, 0)

    rows_np, cols_np = np.triu_indices(nfeat)
    npairs = rows_np.shape[0]
    maxown = (npairs + nblocks - 1) // nblocks
    before = jnp.asarray(np.tril(np.ones((npairs, npairs), np.int32), -1))
    mine = owner == device
    rank = jnp.sum(before * mine.astype(jnp.int32)[None, :], 1)
    selected = mine[None, :] & (rank[None, :] == jnp.arange(maxown)[:, None])
    present = jnp.any(selected, 1)
    row_block = jnp.sum(jnp.where(selected, jnp.asarray(rows_np.astype(np.int32)), 0), 1)
    col_block = jnp.sum(jnp.where(selected, jnp.asarray(cols_np.astype(np.int32)), 0), 1)
    table = jnp.stack([row_block, col_block]).astype(jnp.int32)

    if nblocks == 8 and nframes == 4:
        lanes = quarter // CHUNKS
        raw = [raw[:, k * lanes : (k + 1) * lanes] for k in range(4 * CHUNKS)]
        raw = jnp.stack([jnp.concatenate(raw[h::CHUNKS], 1) for h in range(CHUNKS)])
        total, stats = fused(raw, lag, table, maxown)
        squares = stats[:, :, 2].reshape(nfeat, CHUNKS, 4, lanes)
        squares = squares.transpose(0, 2, 1, 3).reshape(nfeat, BS)
    else:
        gathered, stats = gather_plain(raw, lag[0])
        split = (nfeat, nblocks // nfeat)
        gathered = gathered.reshape(split + gathered.shape[1:])
        gathered = jnp.swapaxes(gathered, 1, 2).reshape(nfeat, WINDOW, BS)
        stats = stats.reshape(split + stats.shape[1:])
        stats = jnp.swapaxes(stats, 1, 2).reshape(nfeat, stats.shape[2], BS)
        full0 = (gathered[:, :SPAN].astype(jnp.float32) - stats[:, 0:1]).astype(jnp.bfloat16)
        full1 = lax.dynamic_slice_in_dim(gathered, lag[0], SPAN, 1).astype(jnp.float32)
        full1 = (full1 - stats[:, 1:2]).astype(jnp.bfloat16)
        squares = stats[:, 2]
        total = owned_products(table, full0, full1, maxown)
    inv = 1.0 / jnp.sqrt(squares + eps)
    total = total.reshape(maxown, 2, quarter, BS)
    mine_inv = lax.dynamic_slice_in_dim(inv, group * quarter, quarter, 1)
    row_inv = jnp.where(present[:, None], jnp.take(mine_inv, row_block, axis=0), 0.0)
    col_inv = jnp.take(inv, col_block, axis=0)
    corr_inst = total[:, 0] * row_inv[:, :, None] * col_inv[:, None, :]
    corr_lag = 0.5 * total[:, 1] * row_inv[:, :, None] * col_inv[:, None, :]
    return (corr_inst.astype(jnp.bfloat16), corr_lag.astype(jnp.bfloat16))


def solution(mesh):
    in_specs = (P("frames", "blocks"), P(), P(), P())
    out_specs = (P("blocks", "frames", None), P("blocks", "frames", None))
    return jax.shard_map(shards, mesh=mesh, in_specs=in_specs, out_specs=out_specs, check_vma=False)
```
